512 devices in a mesh: seq: 128 (over x, y, z_hi, core), tp: 4 (over z_lo).
Axes of the slice: x: 4, y: 8, z: 8 (z_hi: 2, z_lo: 4; z = z_hi * 4 + z_lo), core: 2. Of those that a mesh axis runs over, the one named last changes fastest.
Arguments:
- tokens: bfloat16 [16384, 4096], P('seq')
- norm_gain: float32 [4096], replicated
- qkv_weight: bfloat16 [4096, 3, 2560], P('seq', None, 'tp'), may hold values from -0.09375 to 0.09375
- qkv_keep: int32 [4096, 16], P('seq', 'tp'), may hold values from 0 to 1073741823, as said below
- position_bias: float32 [32, 40], P(None, 'tp'), may hold values from -4 to 4
Outputs:
- context: bfloat16 [16384, 2560], P('seq', 'tp')
The draws below stay inside these ranges and needn't reach their ends.
Inputs may be any that keep to these rules, and one draw needn't show every extreme that they name: `qkv_keep`: bit 10 m + h of word 4 t + j holds the keep flag for columns j * 16 to (j + 1) * 16 - 1 of head 10 t + h of matrix m (0 query, 1 key, 2 value), in the row of the same input feature; bits 30 and 31 are zero. The share of kept flags differs from input feature to input feature, and in every draw all flags of some aligned block of 32 input features are kept.
All inputs are finite; a program needn't handle non-finite values.
Results may differ from the reference program's by a relative error of at most 0.0075.
The reference program's roundings to bfloat16 on the way (of `normed`, `pruned` and `attn_probs`) count: a program that leaves them out, or rounds other values in their place, can miss the bound.
Values may be sent and summed in bfloat16 or wider, within the bound.
No kernel may reach another device: no remote copies, remote signals or barrier semaphores. Data moves between devices by JAX's collectives and lax.ppermute only.
A program may use at most 128 MiB of HBM per device.

```python
import math
import jax
import jax.numpy as jnp
import numpy as np
from jax import lax

D = 4096
HS = 64
RADIUS = 127
NUM_BUCKETS = 32
MAX_DIST = 128
TOK_DEV = 128
HEADS = 40
HD = 2560
TOKENS = 16384
DOC_LEN = 16384
MASK_WORDS = 16
N_SEQ = 128


def draw_tokens(key, part):
    key_one, key_two, key_three = jax.random.split(key, 3)
    noise = jax.random.normal(key_one, (TOKENS, D), jnp.float32)
    column_scale = jnp.exp(jax.random.uniform(key_two, (1, D), jnp.float32, math.log(0.3), math.log(3.0)))
    row_scale = jnp.exp(jax.random.uniform(key_three, (TOKENS, 1), jnp.float32, math.log(0.5), math.log(5.0)))
    return (noise * column_scale * row_scale).astype(jnp.bfloat16)


def draw_norm_gain(key, part):
    values_drawn = jax.random.uniform(key, (D,), jnp.float32, 0.6, 1.5)
    return values_drawn


def draw_qkv_keep(key, part):
    key_level = jax.random.fold_in(key, 11)
    key_coins = jax.random.fold_in(key, 12)
    key_slab = jax.random.fold_in(key, 13)
    level = jax.random.randint(key_level, (D, 1, 1), 1, 17, dtype=jnp.int32)
    coins = jax.random.randint(key_coins, (D, MASK_WORDS, 30), 0, 16, dtype=jnp.int32)
    keep_bits = (coins < level).astype(jnp.int32)
    slab_rows = D // N_SEQ
    full_slab = jax.random.randint(key_slab, (), 0, N_SEQ, dtype=jnp.int32)
    row_slab = jnp.arange(D, dtype=jnp.int32) // slab_rows
    keep_bits = jnp.where((row_slab == full_slab)[:, None, None], jnp.int32(1), keep_bits)
    weights = jnp.left_shift(jnp.int32(1), jnp.arange(30, dtype=jnp.int32))
    return jnp.sum(keep_bits * weights, axis=2).astype(jnp.int32)


def levels(own_key, shape, cuts, smallest, high):
    level, own = 1.0, jax.random.fold_in(own_key, 6)
    for axis_at, blocks in cuts:
        steps = jnp.exp(jax.random.uniform(jax.random.fold_in(own, axis_at), (blocks,), jnp.float32, smallest / len(cuts), high / len(cuts)))
        level = level * jnp.repeat(steps, shape[axis_at] // blocks).reshape([-1 if axis == axis_at else 1 for axis in range(len(shape))])
    return level


def gaussian(rng, shape, scale, reach, shards=(), kind=jnp.bfloat16):
    result = jax.random.normal(rng, shape, jnp.float32) * scale
    if len(shards) > 0:
        result = levels(rng, shape, shards, -0.22, 0.18) * result
    return jnp.clip(result, min=-reach, max=reach).astype(kind)


def setup_inputs(seed: int = 0) -> dict:
    keys = jax.random.split(jax.random.key(seed), 6)
    return {
        "tokens": draw_tokens(jax.random.fold_in(keys[5], 71), 0),
        "norm_gain": draw_norm_gain(jax.random.fold_in(keys[5], 71), 0),
        "qkv_weight": gaussian(keys[2], (D, 3, HD), D ** -0.5, 0.09375, ((0, 128), (2, 4))),
        "qkv_keep": draw_qkv_keep(jax.random.fold_in(keys[5], 71), 0),
        "position_bias": gaussian(keys[4], (NUM_BUCKETS, HEADS), 1.0, 4.0, ((1, 4),), jnp.float32),
    }


def buckets(offsets):
    offsets = np.asarray(offsets, np.int64)
    half_count = NUM_BUCKETS // 2
    sign_part = (offsets > 0).astype(np.int64) * half_count
    distance = np.abs(offsets)
    exact_count = half_count // 2
    log_bucket = exact_count + (np.log(np.maximum(distance, 1) / exact_count) / np.log(MAX_DIST / exact_count) * (half_count - exact_count)).astype(np.int64)
    log_bucket = np.minimum(log_bucket, half_count - 1)
    return sign_part + np.where(distance < exact_count, distance, log_bucket)

def unpack_keep(packed_words, block_width):
    row_count = packed_words.shape[0]
    group_count = packed_words.shape[1] // 4
    shaped = packed_words.reshape(row_count, group_count, 4, 1)
    shifts = jnp.arange(30, dtype=jnp.int32)
    keep_bits = jnp.bitwise_and(jnp.right_shift(shaped, shifts), 1)
    keep_bits = keep_bits.reshape(row_count, group_count, 4, 3, 10)
    keep_bits = jnp.transpose(keep_bits, (0, 3, 1, 4, 2))
    keep_bits = jnp.broadcast_to(keep_bits[..., None], keep_bits.shape + (block_width,))
    return keep_bits.reshape(row_count, 3, group_count * 10 * 4 * block_width)

def reference(tokens, norm_gain, qkv_weight, qkv_keep, position_bias):
    xfloat = tokens.astype(jnp.float32)
    meansq = lax.optimization_barrier(jnp.mean(xfloat * xfloat, axis=1, keepdims=True))
    normed = (xfloat * lax.rsqrt(meansq + 1e-06) * norm_gain).astype(jnp.bfloat16)
    keep_mask = unpack_keep(qkv_keep, HS // 4).astype(jnp.bfloat16)
    pruned = qkv_weight * keep_mask
    projected = jnp.dot(normed, pruned.reshape(D, 3 * HD), preferred_element_type=jnp.float32).astype(jnp.bfloat16)
    queries = projected[:, :HD]
    keys_now = projected[:, HD:2 * HD]
    values_now = projected[:, 2 * HD:]
    padded_keys = jnp.pad(keys_now, ((RADIUS, RADIUS), (0, 0)))
    padded_values = jnp.pad(values_now, ((RADIUS, RADIUS), (0, 0)))
    key_span = TOK_DEV + 2 * RADIUS
    offsets = np.arange(key_span)[None, :] - RADIUS - np.arange(TOK_DEV)[:, None]
    bucket_index = buckets(offsets)
    bias_block = jnp.transpose(position_bias[bucket_index], (2, 0, 1))
    in_reach = jnp.asarray(np.abs(offsets) <= RADIUS)

    def one_block(block_index):
        block_start = block_index * TOK_DEV
        query_rows = lax.dynamic_slice_in_dim(queries, block_start, TOK_DEV, 0).reshape(TOK_DEV, HEADS, HS)
        key_rows = lax.dynamic_slice_in_dim(padded_keys, block_start, key_span, 0).reshape(key_span, HEADS, HS)
        value_rows = lax.dynamic_slice_in_dim(padded_values, block_start, key_span, 0).reshape(key_span, HEADS, HS)
        query_pos = block_start + jnp.arange(TOK_DEV, dtype=jnp.int32)
        key_pos = block_start - RADIUS + jnp.arange(key_span, dtype=jnp.int32)
        allowed = in_reach & (query_pos[:, None] // DOC_LEN == key_pos[None, :] // DOC_LEN)
        allowed = allowed & (key_pos >= 0)[None, :] & (key_pos < TOKENS)[None, :]
        scores = jnp.einsum('qhd,khd->hqk', query_rows.astype(jnp.float32), key_rows.astype(jnp.float32)) + bias_block
        scores = jnp.where(allowed[None], scores, jnp.float32(-1000000000.0))
        row_max = lax.optimization_barrier(jnp.max(scores, axis=2, keepdims=True))
        exp_scores = jnp.exp(scores - row_max)
        row_sum = lax.optimization_barrier(jnp.sum(exp_scores, axis=2, keepdims=True))
        attn_probs = (exp_scores / row_sum).astype(jnp.bfloat16)
        context = jnp.einsum('hqk,khd->qhd', attn_probs.astype(jnp.float32), value_rows.astype(jnp.float32))
        return context.astype(jnp.bfloat16).reshape(TOK_DEV, HD)
    blocks = lax.map(one_block, jnp.arange(N_SEQ, dtype=jnp.int32))
    return blocks.reshape(TOKENS, HD)
```

```python
import functools

import jax
import jax.numpy as jnp
import numpy as np
from jax import lax
from jax.experimental import pallas as pl
from jax.experimental.pallas import tpu as pltpu
from jax.sharding import Mesh, PartitionSpec as P

HS = 64
RADIUS = 127
NUM_BUCKETS = 32
MAX_DIST = 128
LANES = 128
TOK = 128
NX, NY, NZ, NC, NT = 4, 8, 2, 2, 4
SEQ = ("x", "y", "zh", "c")
NEG = -1000000000.0
QUARTER = 512
VMEM = pl.BlockSpec(memory_space=pltpu.VMEM)
SMEM = pl.BlockSpec(memory_space=pltpu.SMEM)
ANY = pl.BlockSpec(memory_space=pl.ANY)


def buckets(offsets):
    offsets = np.asarray(offsets, np.int64)
    half_count = NUM_BUCKETS // 2
    sign_part = (offsets > 0).astype(np.int64) * half_count
    distance = np.abs(offsets)
    exact_count = half_count // 2
    log_bucket = exact_count + (
        np.log(np.maximum(distance, 1) / exact_count)
        / np.log(MAX_DIST / exact_count)
        * (half_count - exact_count)
    ).astype(np.int64)
    log_bucket = np.minimum(log_bucket, half_count - 1)
    return sign_part + np.where(distance < exact_count, distance, log_bucket)


def params(mib=24):
    return pltpu.CompilerParams(vmem_limit_bytes=mib * 1024 * 1024)


def prune_kernel(weight, keep, out):
    rows, cols = weight.shape[1:]
    words = keep[...].T
    lane = lax.broadcasted_iota(jnp.int32, (rows, cols), 1)
    part, head = (lane >> 4) & 3, lane >> 6
    word = jnp.broadcast_to(words[:, 3:4], (rows, cols))
    for j in range(3):
        word = jnp.where(part == j, words[:, j : j + 1], word)
    tiles = cols // LANES
    for place, matrix in enumerate((1, 2, 0)):
        flag = (word >> (head + 10 * matrix)) & 1
        kept = weight[matrix].astype(jnp.float32) * flag.astype(jnp.float32)
        kept = kept.astype(jnp.bfloat16)
        for tile in range(tiles):
            at = place * tiles + tile
            out[at // 4, :, (at % 4) * LANES : (at % 4 + 1) * LANES] = kept[
                :, tile * LANES : (tile + 1) * LANES
            ]
    out[3, :, 3 * LANES :] = jnp.zeros((rows, LANES), jnp.bfloat16)


def prune(weight, keep):
    rows = weight.shape[0]
    return pl.pallas_call(
        prune_kernel,
        out_shape=jax.ShapeDtypeStruct((4, rows, QUARTER), jnp.bfloat16),
        in_specs=[VMEM, VMEM],
        out_specs=VMEM,
        compiler_params=params(),
        name="prune",
    )(jnp.transpose(weight, (1, 0, 2)), keep.T)


def join_kernel(first, second, after, out):
    del after
    rows = first.shape[1]
    out[:, :rows] = first[...]
    out[:, rows:] = second[...]


def join(first, second, after):
    quarters, rows, cols = first.shape
    return pl.pallas_call(
        join_kernel,
        out_shape=jax.ShapeDtypeStruct((quarters, 2 * rows, cols), first.dtype),
        in_specs=[VMEM, VMEM, ANY],
        out_specs=VMEM,
        compiler_params=params(),
        name="join",
    )(first, second, after)


def norm_kernel(tokens, gain, out):
    value = tokens[...].astype(jnp.float32)
    meansq = jnp.mean(value * value, axis=1, keepdims=True)
    out[...] = (value * lax.rsqrt(meansq + 1e-06) * gain[...]).astype(jnp.bfloat16)


def norm(tokens, gain):
    rows, width = tokens.shape
    step = 32
    return pl.pallas_call(
        norm_kernel,
        out_shape=jax.ShapeDtypeStruct((rows, width), jnp.bfloat16),
        grid=(rows // step,),
        in_specs=[
            pl.BlockSpec((step, width), lambda i: (i, 0)),
            pl.BlockSpec((1, width), lambda i: (0, 0)),
        ],
        out_specs=pl.BlockSpec((step, width), lambda i: (i, 0)),
        compiler_params=params(),
        name="norm",
    )(tokens, gain.reshape(1, width))


def bias_kernel(line, out):
    for head in range(line.shape[0]):
        block = jnp.broadcast_to(line[head : head + 1, :], out.shape[1:])
        out[head] = pltpu.roll(block, 0, 1, stride=1, stride_axis=0)


def bias_blocks(position_bias):
    heads = position_bias.shape[1]
    offsets = np.arange(3 * TOK) - TOK
    onehot = buckets(offsets)[None, :] == np.arange(NUM_BUCKETS)[:, None]
    line = jnp.dot(
        position_bias.T,
        jnp.asarray(onehot.astype(np.float32)),
        precision=lax.Precision.HIGHEST,
    )
    return pl.pallas_call(
        bias_kernel,
        out_shape=jax.ShapeDtypeStruct((heads, TOK, 3 * TOK), jnp.float32),
        in_specs=[VMEM],
        out_specs=VMEM,
        compiler_params=params(),
        name="bias",
    )(line)


def project_kernel(at, own, one, two, three, weight, out, toks, rows, total, tok_sem, row_sem):
    x, zh = at[0], at[1]
    copies = []
    for d, ref in enumerate((own, one, two, three)):
        copies.append(
            pltpu.make_async_copy(ref, toks.at[pl.ds(d * TOK, TOK), :], tok_sem.at[d])
        )
    loads = []
    for block in range(NX):
        for z in range(NZ):
            loads.append(
                pltpu.make_async_copy(
                    weight.at[:, :, block, lax.rem(z + zh, 2)],
                    rows.at[block, :, z],
                    row_sem.at[block, z],
                )
            )
    for copy in loads[:2] + copies + loads[2:]:
        copy.start()
    for copy in copies:
        copy.wait()
    depth = toks.shape[1] // NX
    for block in range(NX):
        loads[2 * block].wait()
        loads[2 * block + 1].wait()
        product = jnp.dot(
            toks[:, block * depth : (block + 1) * depth],
            rows[block].reshape(depth, QUARTER),
            preferred_element_type=jnp.float32,
        )
        if block == 0:
            total[...] = product
        elif block < NX - 1:
            total[...] += product
        else:
            product = (total[...] + product).astype(jnp.bfloat16)
            for d in range(NX):
                out[lax.rem(x + NX - d, NX)] = product[d * TOK : (d + 1) * TOK]


def project(at, blocks, weight):
    width = blocks[0].shape[1]
    return pl.pallas_call(
        project_kernel,
        out_shape=jax.ShapeDtypeStruct((NX, TOK, QUARTER), jnp.bfloat16),
        in_specs=[SMEM] + [ANY] * 5,
        out_specs=VMEM,
        scratch_shapes=[
            pltpu.VMEM((NX * TOK, width), jnp.bfloat16),
            pltpu.VMEM((NX, NY, NZ, NC, 32, QUARTER), jnp.bfloat16),
            pltpu.VMEM((NX * TOK, QUARTER), jnp.float32),
            pltpu.SemaphoreType.DMA((NX,)),
            pltpu.SemaphoreType.DMA((NX, NZ)),
        ],
        compiler_params=params(24),
        cost_estimate=pl.CostEstimate(
            flops=2 * NX * TOK * width * QUARTER, bytes_accessed=10 << 20, transcendentals=0
        ),
        name="project",
    )(at, *blocks, weight.reshape(NY, NC, NX, NZ, 32, QUARTER))


def attend_kernel(at, own, before, after, bias, out):
    seq = at[0]
    heads = bias.shape[0]
    tiles = heads // 2
    column = lax.broadcasted_iota(jnp.int32, (1, 3 * TOK), 1)
    shut = ((column < TOK) & (seq == 0)) | ((column >= 2 * TOK) & (seq == at[1]))
    near = jnp.abs(column - TOK - lax.broadcasted_iota(jnp.int32, (TOK, 3 * TOK), 0)) <= RADIUS
    allowed = near & ~shut
    lane = lax.broadcasted_iota(jnp.int32, (TOK, LANES), 1)
    low = lane < HS

    def tile_of(tile):
        return own[tile // 4, :, (tile % 4) * LANES : (tile % 4 + 1) * LANES]

    def extended(tile):
        cut = slice(tile * LANES, (tile + 1) * LANES)
        return jnp.concatenate([before[:, cut], tile_of(tile), after[:, cut]], axis=0)

    for tile in range(tiles):
        keys, values, query = extended(tile), extended(tiles + tile), tile_of(2 * tiles + tile)
        results = []
        for half in range(2):
            picked = jnp.where(low if half == 0 else ~low, query, jnp.zeros_like(query))
            scores = lax.dot_general(
                picked, keys, (((1,), (1,)), ((), ())), preferred_element_type=jnp.float32
            )
            scores = jnp.where(allowed, scores + bias[2 * tile + half], jnp.float32(NEG))
            top = jnp.max(scores, axis=1, keepdims=True)
            weights = jnp.exp(scores - top)
            share = 1.0 / jnp.sum(weights, axis=1, keepdims=True)
            probs = (weights * share).astype(jnp.bfloat16)
            results.append(jnp.dot(probs, values, preferred_element_type=jnp.float32))
        out[:, tile * LANES : (tile + 1) * LANES] = jnp.where(low, *results).astype(jnp.bfloat16)


def attend(at, own, before, after, bias):
    heads = bias.shape[0]
    return pl.pallas_call(
        attend_kernel,
        out_shape=jax.ShapeDtypeStruct((TOK, heads * HS), jnp.bfloat16),
        in_specs=[SMEM] + [VMEM] * 4,
        out_specs=VMEM,
        compiler_params=params(),
        name="attend",
    )(at, own, before, after, bias)


def shifted(count, step):
    return [(i, (i + step) % count) for i in range(count)]


def body(tokens, norm_gain, qkv_weight, qkv_keep, position_bias):
    x, zh = lax.axis_index("x"), lax.axis_index("zh")
    seq, last = lax.axis_index(SEQ), lax.axis_size(SEQ) - 1
    pruned = prune(qkv_weight, qkv_keep)
    swapped = lax.ppermute(pruned, "zh", shifted(NZ, 1))
    normed = norm(tokens, norm_gain)
    blocks = [normed] + [lax.ppermute(normed, "x", shifted(NX, d)) for d in (1, 2, 3)]
    both = join(pruned, swapped, normed)
    mine = lax.all_to_all(both, "x", 0, 0, tiled=True)
    gathered = lax.all_gather(mine.reshape(-1, QUARTER), ("y", "c"), axis=0, tiled=True)
    bias = bias_blocks(position_bias)
    projected = project(jnp.stack([x, zh]).astype(jnp.int32), blocks, gathered)
    own = lax.all_to_all(projected, "x", 0, 0, tiled=True)
    edges = jnp.concatenate([own[0], own[1], own[2][:, : QUARTER // 2]], axis=1)
    before = lax.ppermute(edges, SEQ, [(i, i + 1) for i in range(last)])
    after = lax.ppermute(edges, SEQ, [(i + 1, i) for i in range(last)])
    return attend(jnp.stack([seq, last]).astype(jnp.int32), own, before, after, bias)


def solution(mesh):
    grid = Mesh(mesh.devices.reshape(NX, NY, NZ, NC, NT), SEQ + ("tp",))
    return jax.shard_map(
        body,
        mesh=grid,
        in_specs=(P(SEQ, None), P(), P(SEQ, None, "tp"), P(SEQ, "tp"), P(None, "tp")),
        out_specs=P(SEQ, "tp"),
        check_vma=False,
    )
```

```python
import functools

import jax
import jax.numpy as jnp
import numpy as np
from jax import lax
from jax.experimental import pallas as pl
from jax.experimental.pallas import tpu as pltpu
from jax.sharding import Mesh, PartitionSpec as P

HS = 64
RADIUS = 127
NUM_BUCKETS = 32
MAX_DIST = 128
LANES = 128
TOK = 128
NX, NY, NZ, NC, NT = 4, 8, 2, 2, 4
SEQ = ("x", "y", "zh", "c")
QUARTER = 512
VMEM = pl.BlockSpec(memory_space=pltpu.VMEM)
SMEM = pl.BlockSpec(memory_space=pltpu.SMEM)
ANY = pl.BlockSpec(memory_space=pl.ANY)


def buckets(offsets):
    offsets = np.asarray(offsets, np.int64)
    half_count = NUM_BUCKETS // 2
    sign_part = (offsets > 0).astype(np.int64) * half_count
    distance = np.abs(offsets)
    exact_count = half_count // 2
    log_bucket = exact_count + (
        np.log(np.maximum(distance, 1) / exact_count)
        / np.log(MAX_DIST / exact_count)
        * (half_count - exact_count)
    ).astype(np.int64)
    log_bucket = np.minimum(log_bucket, half_count - 1)
    return sign_part + np.where(distance < exact_count, distance, log_bucket)


def params(mib=8):
    return pltpu.CompilerParams(vmem_limit_bytes=mib * 1024 * 1024)


def prune_kernel(weight, keep, out):
    rows, cols = weight.shape[1:]
    words = keep[...].T
    lane = lax.broadcasted_iota(jnp.int32, (rows, cols), 1)
    part, head = (lane >> 4) & 3, lane >> 6
    word = jnp.broadcast_to(words[:, 3:4], (rows, cols))
    for j in range(3):
        word = jnp.where(part == j, words[:, j : j + 1], word)
    tiles = cols // LANES
    for place, matrix in enumerate((1, 2, 0)):
        flag = (word >> (head + 10 * matrix)) & 1
        kept = weight[matrix].astype(jnp.float32) * flag.astype(jnp.float32)
        kept = kept.astype(jnp.bfloat16)
        for tile in range(tiles):
            at = place * tiles + tile
            out[at // 4, :, (at % 4) * LANES : (at % 4 + 1) * LANES] = kept[
                :, tile * LANES : (tile + 1) * LANES
            ]
    out[3, :, 3 * LANES :] = jnp.zeros((rows, LANES), jnp.bfloat16)


def prune(weight, keep):
    rows = weight.shape[0]
    return pl.pallas_call(
        prune_kernel,
        out_shape=jax.ShapeDtypeStruct((4, rows, QUARTER), jnp.bfloat16),
        in_specs=[VMEM, VMEM],
        out_specs=VMEM,
        compiler_params=params(),
        name="prune",
    )(jnp.transpose(weight, (1, 0, 2)), keep.T)


def join_kernel(first, second, after, out):
    del after
    rows = first.shape[1]
    out[:, :rows] = first[...]
    out[:, rows:] = second[...]


def join(first, second, after):
    quarters, rows, cols = first.shape
    return pl.pallas_call(
        join_kernel,
        out_shape=jax.ShapeDtypeStruct((quarters, 2 * rows, cols), first.dtype),
        in_specs=[VMEM, VMEM, ANY],
        out_specs=VMEM,
        compiler_params=params(),
        name="join",
    )(first, second, after)


def norm_kernel(tokens, gain, out):
    value = tokens[...].astype(jnp.float32)
    meansq = jnp.mean(value * value, axis=1, keepdims=True)
    out[...] = (value * lax.rsqrt(meansq + 1e-06) * gain[...]).astype(jnp.bfloat16)


def norm(tokens, gain):
    rows, width = tokens.shape
    step = 32
    return pl.pallas_call(
        norm_kernel,
        out_shape=jax.ShapeDtypeStruct((rows, width), jnp.bfloat16),
        grid=(rows // step,),
        in_specs=[
            pl.BlockSpec((step, width), lambda i: (i, 0)),
            pl.BlockSpec((1, width), lambda i: (0, 0)),
        ],
        out_specs=pl.BlockSpec((step, width), lambda i: (i, 0)),
        compiler_params=params(),
        name="norm",
    )(tokens, gain.reshape(1, width))


def bias_kernel(place, line, out):
    rows, columns = out.shape[1:]
    column = lax.broadcasted_iota(jnp.int32, (rows, columns), 1)
    near = jnp.abs(column - TOK - lax.broadcasted_iota(jnp.int32, (rows, columns), 0)) <= RADIUS
    shut = ((column < TOK) & (place[0] == 0)) | ((column >= 2 * TOK) & (place[0] == place[1]))
    allowed = near & ~shut
    for head in range(line.shape[0]):
        block = jnp.broadcast_to(line[head : head + 1, :], (rows, columns))
        block = pltpu.roll(block, 0, 1, stride=1, stride_axis=0)
        out[head] = jnp.where(allowed, block, -jnp.inf)


def bias_blocks(place, position_bias):
    heads = position_bias.shape[1]
    offsets = np.arange(3 * TOK) - TOK
    onehot = buckets(offsets)[None, :] == np.arange(NUM_BUCKETS)[:, None]
    line = jnp.dot(
        position_bias.T,
        jnp.asarray(onehot.astype(np.float32)),
        precision=lax.Precision.HIGHEST,
    )
    return pl.pallas_call(
        bias_kernel,
        out_shape=jax.ShapeDtypeStruct((heads, TOK, 3 * TOK), jnp.float32),
        in_specs=[SMEM, VMEM],
        out_specs=VMEM,
        compiler_params=params(),
        name="bias",
    )(place, line)


def project_kernel(at, *refs):
    tokens, weight, out = refs[:5], refs[5], refs[6]
    toks, rows, total, tok_sem, row_sem = refs[7:]
    x, zh = at[0], at[1]
    copies, start = [], 0
    for i, ref in enumerate(tokens):
        size = ref.shape[0]
        copies.append(pltpu.make_async_copy(ref, toks.at[pl.ds(start, size)], tok_sem.at[i]))
        start += size
    loads = []
    for block in range(NX):
        for z in range(NZ):
            source = weight.at[:, :, block, lax.rem(z + zh, NZ)]
            sem = row_sem.at[block * NZ + z]
            loads.append(pltpu.make_async_copy(source, rows.at[block, :, z], sem))
    for copy in loads[:2] + copies + loads[2:]:
        copy.start()
    for copy in copies:
        copy.wait()
    depth = toks.shape[1] // NX
    for block in range(NX):
        for load in loads[2 * block : 2 * block + 2]:
            load.wait()
        product = jnp.dot(
            toks[:, block * depth : (block + 1) * depth],
            rows[block].reshape(depth, QUARTER),
            preferred_element_type=jnp.float32,
        )
        if block == 0:
            total[...] = product
        elif block < NX - 1:
            total[...] += product
        else:
            product = (total[...] + product).astype(jnp.bfloat16)
            for d, step in enumerate((0, 3, 1, 2)):
                out[lax.rem(x + step, NX)] = product[d * TOK : (d + 1) * TOK]


def project(at, tokens, weight):
    width = tokens[0].shape[1]
    return pl.pallas_call(
        project_kernel,
        out_shape=jax.ShapeDtypeStruct((NX, TOK, QUARTER), jnp.bfloat16),
        in_specs=[SMEM] + [ANY] * 6,
        out_specs=VMEM,
        scratch_shapes=[
            pltpu.VMEM((NX * TOK, width), jnp.bfloat16),
            pltpu.VMEM((NX, NY, NZ, NC, 32, QUARTER), jnp.bfloat16),
            pltpu.VMEM((NX * TOK, QUARTER), jnp.float32),
            pltpu.SemaphoreType.DMA((5,)),
            pltpu.SemaphoreType.DMA((NX * NZ,)),
        ],
        compiler_params=params(58),
        cost_estimate=pl.CostEstimate(
            flops=2 * NX * TOK * width * QUARTER, bytes_accessed=10 << 20, transcendentals=0
        ),
        name="project",
    )(at, *tokens, weight.reshape(NY, NC, NX, NZ, 32, QUARTER))


def attend_kernel(at, own, inner, outer, bias, out):
    first = at[0] == 0
    heads = bias.shape[0]
    tiles = heads // 2
    lane = lax.broadcasted_iota(jnp.int32, (TOK, LANES), 1)
    low = lane < HS

    def tile_of(tile):
        return own[tile // 4, :, (tile % 4) * LANES : (tile % 4 + 1) * LANES]

    def extended(tile):
        cut = slice(tile * LANES, (tile + 1) * LANES)
        before = jnp.where(first, outer[:, cut], inner[0, :, cut])
        after = jnp.where(first, inner[1, :, cut], outer[:, cut])
        return jnp.concatenate([before, tile_of(tile), after], axis=0)

    for tile in range(tiles):
        keys, values, query = extended(tile), extended(tiles + tile), tile_of(2 * tiles + tile)
        results = []
        for half in range(2):
            picked = jnp.where(low if half == 0 else ~low, query, jnp.zeros_like(query))
            scores = lax.dot_general(
                picked, keys, (((1,), (1,)), ((), ())), preferred_element_type=jnp.float32
            )
            scores = scores + bias[2 * tile + half]
            top = jnp.max(scores, axis=1, keepdims=True)
            weights = jnp.exp(scores - top)
            share = 1.0 / jnp.sum(weights, axis=1, keepdims=True)
            probs = (weights * share).astype(jnp.bfloat16)
            results.append(jnp.dot(probs, values, preferred_element_type=jnp.float32))
        out[:, tile * LANES : (tile + 1) * LANES] = jnp.where(low, *results).astype(jnp.bfloat16)


def attend(at, own, inner, outer, bias):
    heads = bias.shape[0]
    return pl.pallas_call(
        attend_kernel,
        out_shape=jax.ShapeDtypeStruct((TOK, heads * HS), jnp.bfloat16),
        in_specs=[SMEM] + [VMEM] * 4,
        out_specs=VMEM,
        compiler_params=params(),
        name="attend",
    )(at, own, inner, outer, bias)


def shifted(count, step):
    return [(i, (i + step) % count) for i in range(count)]


def body(tokens, norm_gain, qkv_weight, qkv_keep, position_bias):
    x, zh, c = (lax.axis_index(name) for name in ("x", "zh", "c"))
    seq, last = lax.axis_index(SEQ), lax.axis_size(SEQ) - 1
    pruned = prune(qkv_weight, qkv_keep)
    swapped = lax.ppermute(pruned, "zh", shifted(NZ, 1))
    normed = norm(tokens, norm_gain)
    behind, ahead = (lax.ppermute(normed, "x", shifted(NX, d)) for d in (1, 3))
    half = normed.shape[0] // 2
    far = [lax.ppermute(behind[:half], "x", shifted(NX, 1))]
    far += [lax.ppermute(ahead[half:], "x", shifted(NX, 3))]
    both = join(pruned, swapped, normed)
    mine = lax.all_to_all(both, "x", 0, 0, tiled=True)
    gathered = lax.all_gather(mine.reshape(-1, QUARTER), ("y", "c"), axis=0, tiled=True)
    bias = bias_blocks(jnp.stack([seq, jnp.int32(last)]).astype(jnp.int32), position_bias)
    at = jnp.stack([x, zh]).astype(jnp.int32)
    projected = project(at, [normed, behind, ahead, *far], gathered)
    own = lax.all_to_all(projected, "x", 0, 0, tiled=True)
    edges = jnp.concatenate([own[0], own[1], own[2][:, : QUARTER // 2]], axis=1)
    inner = lax.all_gather(edges, "c")
    pairs = [(i, i + 1) for i in range(1, last, 2)]
    outer = lax.ppermute(edges, SEQ, pairs + [(j, i) for i, j in pairs])
    return attend(c.reshape(1).astype(jnp.int32), own, inner, outer, bias)


def solution(mesh):
    grid = Mesh(mesh.devices.reshape(NX, NY, NZ, NC, NT), SEQ + ("tp",))
    return jax.shard_map(
        body,
        mesh=grid,
        in_specs=(P(SEQ, None), P(), P(SEQ, None, "tp"), P(SEQ, "tp"), P(None, "tp")),
        out_specs=P(SEQ, "tp"),
        check_vma=False,
    )
```

```python
import functools

import jax
import jax.numpy as jnp
import numpy as np
from jax import lax
from jax.experimental import pallas as pl
from jax.experimental.pallas import tpu as pltpu
from jax.sharding import Mesh, PartitionSpec as P

HS = 64
RADIUS = 127
NUM_BUCKETS = 32
MAX_DIST = 128
LANES = 128
TOK = 128
NX, NY, NZ, NC, NT = 4, 8, 2, 2, 4
SEQ = ("x", "y", "zh", "c")
QUARTER = 512
VMEM = pl.BlockSpec(memory_space=pltpu.VMEM)
SMEM = pl.BlockSpec(memory_space=pltpu.SMEM)
ANY = pl.BlockSpec(memory_space=pl.ANY)


def buckets(offsets):
    offsets = np.asarray(offsets, np.int64)
    half_count = NUM_BUCKETS // 2
    sign_part = (offsets > 0).astype(np.int64) * half_count
    distance = np.abs(offsets)
    exact_count = half_count // 2
    log_bucket = exact_count + (
        np.log(np.maximum(distance, 1) / exact_count)
        / np.log(MAX_DIST / exact_count)
        * (half_count - exact_count)
    ).astype(np.int64)
    log_bucket = np.minimum(log_bucket, half_count - 1)
    return sign_part + np.where(distance < exact_count, distance, log_bucket)


def params(mib=8):
    return pltpu.CompilerParams(vmem_limit_bytes=mib * 1024 * 1024)


def prune_kernel(given_weight, given_keep, out, weight, keep, sem):
    copies = [
        pltpu.make_async_copy(given_keep, keep, sem.at[0]),
        pltpu.make_async_copy(given_weight, weight, sem.at[1]),
    ]
    for copy in copies:
        copy.start()
    for copy in copies:
        copy.wait()
    rows, cols = weight.shape[1:]
    words = keep[...].T
    lane = lax.broadcasted_iota(jnp.int32, (rows, cols), 1)
    part, head = (lane >> 4) & 3, lane >> 6
    word = jnp.broadcast_to(words[:, 3:4], (rows, cols))
    for j in range(3):
        word = jnp.where(part == j, words[:, j : j + 1], word)
    tiles = cols // LANES
    for place, matrix in enumerate((1, 2, 0)):
        flag = (word >> (head + 10 * matrix)) & 1
        kept = weight[matrix].astype(jnp.float32) * flag.astype(jnp.float32)
        kept = kept.astype(jnp.bfloat16)
        for tile in range(tiles):
            at = place * tiles + tile
            out[at // 4, :, (at % 4) * LANES : (at % 4 + 1) * LANES] = kept[
                :, tile * LANES : (tile + 1) * LANES
            ]
    out[3, :, 3 * LANES :] = jnp.zeros((rows, LANES), jnp.bfloat16)


def prune(weight, keep):
    rows = weight.shape[0]
    return pl.pallas_call(
        prune_kernel,
        out_shape=jax.ShapeDtypeStruct((4, rows, QUARTER), jnp.bfloat16),
        in_specs=[ANY, ANY],
        out_specs=VMEM,
        scratch_shapes=[
            pltpu.VMEM((3, rows, weight.shape[2]), weight.dtype),
            pltpu.VMEM((keep.shape[1], rows), keep.dtype),
            pltpu.SemaphoreType.DMA((2,)),
        ],
        compiler_params=params(),
        name="prune",
    )(jnp.transpose(weight, (1, 0, 2)), keep.T)


def norm_kernel(tokens, gain, after, out):
    del after
    value = tokens[...].astype(jnp.float32)
    meansq = jnp.mean(value * value, axis=1, keepdims=True)
    out[...] = (value * lax.rsqrt(meansq + 1e-06) * gain[...]).astype(jnp.bfloat16)


def norm(tokens, gain, after):
    rows, width = tokens.shape
    step = 32
    return pl.pallas_call(
        norm_kernel,
        out_shape=jax.ShapeDtypeStruct((rows, width), jnp.bfloat16),
        grid=(rows // step,),
        in_specs=[
            pl.BlockSpec((step, width), lambda i: (i, 0)),
            pl.BlockSpec((1, width), lambda i: (0, 0)),
            ANY,
        ],
        out_specs=pl.BlockSpec((step, width), lambda i: (i, 0)),
        compiler_params=params(),
        name="norm",
    )(tokens, gain.reshape(1, width), after)


def bias_kernel(place, line, out):
    rows, columns = out.shape[1:]
    column = lax.broadcasted_iota(jnp.int32, (rows, columns), 1)
    near = jnp.abs(column - TOK - lax.broadcasted_iota(jnp.int32, (rows, columns), 0)) <= RADIUS
    shut = ((column < TOK) & (place[0] == 0)) | ((column >= 2 * TOK) & (place[0] == place[1]))
    allowed = near & ~shut
    for head in range(line.shape[0]):
        block = jnp.broadcast_to(line[head : head + 1, :], (rows, columns))
        block = pltpu.roll(block, 0, 1, stride=1, stride_axis=0)
        out[head] = jnp.where(allowed, block, -jnp.inf)


def bias_blocks(place, position_bias):
    heads = position_bias.shape[1]
    offsets = np.arange(3 * TOK) - TOK
    onehot = buckets(offsets)[None, :] == np.arange(NUM_BUCKETS)[:, None]
    line = jnp.dot(
        position_bias.T,
        jnp.asarray(onehot.astype(np.float32)),
        precision=lax.Precision.HIGHEST,
    )
    return pl.pallas_call(
        bias_kernel,
        out_shape=jax.ShapeDtypeStruct((heads, TOK, 3 * TOK), jnp.float32),
        in_specs=[SMEM, VMEM],
        out_specs=VMEM,
        compiler_params=params(),
        name="bias",
    )(place, line)


def project_kernel(at, *refs):
    tokens, weight, out = refs[:5], refs[5], refs[6]
    toks, rows, total, tok_sem, row_sem = refs[7:]
    x = at[0]
    depth = toks.shape[1] // NX
    copies = []
    for block in range(NX):
        start = 0
        cut = pl.ds(block * depth, depth)
        for i, ref in enumerate(tokens):
            size = ref.shape[0]
            target = toks.at[pl.ds(start, size), cut]
            copies.append(pltpu.make_async_copy(ref.at[:, cut], target, tok_sem.at[block, i]))
            start += size
        for z in range(NZ):
            source = weight.at[:, :, block, z]
            copies.append(
                pltpu.make_async_copy(source, rows.at[block, :, z], row_sem.at[block, z])
            )
    for copy in copies:
        copy.start()
    for block in range(NX):
        for copy in copies[7 * block : 7 * block + 7]:
            copy.wait()
        product = jnp.dot(
            toks[:, block * depth : (block + 1) * depth],
            rows[block].reshape(depth, QUARTER),
            preferred_element_type=jnp.float32,
        )
        if block == 0:
            total[...] = product
        elif block < NX - 1:
            total[...] += product
        else:
            product = (total[...] + product).astype(jnp.bfloat16)
            for d, step in enumerate((0, 3, 1, 2)):
                out[lax.rem(x + step, NX)] = product[d * TOK : (d + 1) * TOK]


def project(at, tokens, weight):
    width = tokens[0].shape[1]
    return pl.pallas_call(
        project_kernel,
        out_shape=jax.ShapeDtypeStruct((NX, TOK, QUARTER), jnp.bfloat16),
        in_specs=[SMEM] + [ANY] * 6,
        out_specs=VMEM,
        scratch_shapes=[
            pltpu.VMEM((NX * TOK, width), jnp.bfloat16),
            pltpu.VMEM((NX, NY, NZ, NC, 32, QUARTER), jnp.bfloat16),
            pltpu.VMEM((NX * TOK, QUARTER), jnp.float32),
            pltpu.SemaphoreType.DMA((NX, 5)),
            pltpu.SemaphoreType.DMA((NX, NZ)),
        ],
        compiler_params=params(58),
        cost_estimate=pl.CostEstimate(
            flops=2 * NX * TOK * width * QUARTER, bytes_accessed=10 << 20, transcendentals=0
        ),
        name="project",
    )(at, *tokens, weight.reshape(NY, NC, NX, NZ, 32, QUARTER))


def own_tile(own, tile):
    return own[tile // 4, :, (tile % 4) * LANES : (tile % 4 + 1) * LANES]


def pair_scores(own, keys, bias, pair, tiles):
    query = own_tile(own, 2 * tiles + pair)
    low = lax.broadcasted_iota(jnp.int32, query.shape, 1) < HS
    for half in range(2):
        picked = jnp.where(low if half == 0 else ~low, query, jnp.zeros_like(query))
        scores = lax.dot_general(
            picked, keys, (((1,), (1,)), ((), ())), preferred_element_type=jnp.float32
        )
        yield scores + bias(2 * pair + half)


def near_kernel(at, own, inner, bias, sums, total, top):
    c = at[0]
    tiles = bias.shape[0] // 2
    low = lax.broadcasted_iota(jnp.int32, (TOK, LANES), 1) < HS
    there = pl.multiple_of((1 - c) * 2 * TOK, TOK)

    def both(tile):
        cut = slice(tile * LANES, (tile + 1) * LANES)
        return jnp.concatenate([own_tile(own, tile), inner[1 - c, :, cut]], axis=0)

    def near_bias(head):
        return jnp.concatenate(
            [bias[head, :, TOK : 2 * TOK], bias[head, :, pl.ds(there, TOK)]], axis=1
        )

    for pair in range(tiles):
        keys, values, results = both(pair), both(tiles + pair), []
        for half, scores in enumerate(pair_scores(own, keys, near_bias, pair, tiles)):
            greatest = jnp.max(scores, axis=1, keepdims=True)
            weights = jnp.exp(scores - greatest)
            top[2 * pair + half] = jnp.broadcast_to(greatest, (TOK, LANES))
            total[2 * pair + half] = jnp.broadcast_to(
                jnp.sum(weights, axis=1, keepdims=True), (TOK, LANES)
            )
            results.append(
                jnp.dot(weights.astype(jnp.bfloat16), values, preferred_element_type=jnp.float32)
            )
        sums[:, pair * LANES : (pair + 1) * LANES] = jnp.where(low, *results)


def attend_kernel(at, own, outer, bias, sums, total, top, out, held, sem):
    copies = []
    c = at[0]
    tiles = bias.shape[0] // 2
    low = lax.broadcasted_iota(jnp.int32, (TOK, LANES), 1) < HS
    there = pl.multiple_of(c * 2 * TOK, TOK)
    for pair in range(tiles):
        cut = slice(pair * LANES, (pair + 1) * LANES)
        keys = outer[:, cut]
        values = outer[:, (tiles + pair) * LANES : (tiles + pair + 1) * LANES]
        scales, totals, results = [], [], []
        far_bias = lambda head: bias[head, :, pl.ds(there, TOK)]
        for half, scores in enumerate(pair_scores(own, keys, far_bias, pair, tiles)):
            head = 2 * pair + half
            greatest = jnp.maximum(top[head], jnp.max(scores, axis=1, keepdims=True))
            weights = jnp.exp(scores - greatest)
            scales.append(jnp.exp(top[head] - greatest))
            totals.append(total[head] * scales[-1] + jnp.sum(weights, axis=1, keepdims=True))
            results.append(
                jnp.dot(weights.astype(jnp.bfloat16), values, preferred_element_type=jnp.float32)
            )
        summed = sums[:, cut] * jnp.where(low, *scales) + jnp.where(low, *results)
        held[:, cut] = (summed / jnp.where(low, *totals)).astype(jnp.bfloat16)
        copies.append(pltpu.make_async_copy(held.at[:, cut], out.at[:, cut], sem.at[pair]))
        copies[-1].start()
    for copy in copies:
        copy.wait()


def attend(core, own, inner, outer, bias):
    heads = bias.shape[0]
    row = jax.ShapeDtypeStruct((heads, TOK, LANES), jnp.float32)
    near = pl.pallas_call(
        near_kernel,
        out_shape=[jax.ShapeDtypeStruct((TOK, heads * HS), jnp.float32), row, row],
        in_specs=[SMEM] + [VMEM] * 3,
        out_specs=[VMEM] * 3,
        compiler_params=params(),
        name="near",
    )(core, own, inner, bias)
    return pl.pallas_call(
        attend_kernel,
        out_shape=jax.ShapeDtypeStruct((TOK, heads * HS), jnp.bfloat16),
        in_specs=[SMEM] + [VMEM] * 6,
        out_specs=ANY,
        scratch_shapes=[
            pltpu.VMEM((TOK, heads * HS), jnp.bfloat16),
            pltpu.SemaphoreType.DMA((heads // 2,)),
        ],
        compiler_params=params(),
        name="attend",
    )(core, own, outer, bias, *near)


def shifted(count, step):
    return [(i, (i + step) % count) for i in range(count)]


def body(tokens, norm_gain, qkv_weight, qkv_keep, position_bias):
    x, c = lax.axis_index("x"), lax.axis_index("c")
    seq, last = lax.axis_index(SEQ), lax.axis_size(SEQ) - 1
    pruned = prune(qkv_weight, qkv_keep)
    both = lax.all_gather(pruned, "zh", axis=1, tiled=True)
    mine = lax.all_to_all(both, "x", 0, 0, tiled=True)
    normed = norm(tokens, norm_gain, mine)
    behind, ahead = (lax.ppermute(normed, "x", shifted(NX, d)) for d in (1, 3))
    half = normed.shape[0] // 2
    far = [lax.ppermute(behind[:half], "x", shifted(NX, 1))]
    far += [lax.ppermute(ahead[half:], "x", shifted(NX, 3))]
    gathered = lax.all_gather(mine.reshape(-1, QUARTER), ("y", "c"), axis=0, tiled=True)
    bias = bias_blocks(jnp.stack([seq, jnp.int32(last)]).astype(jnp.int32), position_bias)
    at = x.reshape(1).astype(jnp.int32)
    projected = project(at, [normed, behind, ahead, *far], gathered)
    own = lax.all_to_all(projected, "x", 0, 0, tiled=True)
    edges = jnp.concatenate([own[0], own[1], own[2][:, : QUARTER // 2]], axis=1)
    inner = lax.all_gather(edges, "c")
    pairs = [(i, i + 1) for i in range(1, last, 2)]
    outer = lax.ppermute(edges, SEQ, pairs + [(j, i) for i, j in pairs])
    return attend(c.reshape(1).astype(jnp.int32), own, inner, outer, bias)


def solution(mesh):
    grid = Mesh(mesh.devices.reshape(NX, NY, NZ, NC, NT), SEQ + ("tp",))
    return jax.shard_map(
        body,
        mesh=grid,
        in_specs=(P(SEQ, None), P(), P(SEQ, None, "tp"), P(SEQ, "tp"), P(None, "tp")),
        out_specs=P(SEQ, "tp"),
        check_vma=False,
    )
```

```python
import functools

import jax
import jax.numpy as jnp
import numpy as np
from jax import lax
from jax.experimental import pallas as pl
from jax.experimental.pallas import tpu as pltpu
from jax.sharding import Mesh, PartitionSpec as P

HS = 64
RADIUS = 127
NUM_BUCKETS = 32
MAX_DIST = 128
LANES = 128
TOK = 128
NX, NY, NZ, NC, NT = 4, 8, 2, 2, 4
SEQ = ("x", "y", "zh", "c")
QUARTER = 512
VMEM = pl.BlockSpec(memory_space=pltpu.VMEM)
SMEM = pl.BlockSpec(memory_space=pltpu.SMEM)
ANY = pl.BlockSpec(memory_space=pl.ANY)


def buckets(offsets):
    offsets = np.asarray(offsets, np.int64)
    half_count = NUM_BUCKETS // 2
    sign_part = (offsets > 0).astype(np.int64) * half_count
    distance = np.abs(offsets)
    exact_count = half_count // 2
    log_bucket = exact_count + (
        np.log(np.maximum(distance, 1) / exact_count)
        / np.log(MAX_DIST / exact_count)
        * (half_count - exact_count)
    ).astype(np.int64)
    log_bucket = np.minimum(log_bucket, half_count - 1)
    return sign_part + np.where(distance < exact_count, distance, log_bucket)


def params(mib=8):
    return pltpu.CompilerParams(vmem_limit_bytes=mib * 1024 * 1024)


def prune_kernel(given_weight, given_keep, out, weight, keep, sem):
    copies = [
        pltpu.make_async_copy(given_keep, keep, sem.at[0]),
        pltpu.make_async_copy(given_weight, weight, sem.at[1]),
    ]
    for copy in copies:
        copy.start()
    for copy in copies:
        copy.wait()
    rows, cols = weight.shape[1:]
    words = keep[...].T
    lane = lax.broadcasted_iota(jnp.int32, (rows, cols), 1)
    part, head = (lane >> 4) & 3, lane >> 6
    word = jnp.broadcast_to(words[:, 3:4], (rows, cols))
    for j in range(3):
        word = jnp.where(part == j, words[:, j : j + 1], word)
    tiles = cols // LANES
    for place, matrix in enumerate((1, 2, 0)):
        flag = (word >> (head + 10 * matrix)) & 1
        kept = weight[matrix].astype(jnp.float32) * flag.astype(jnp.float32)
        kept = kept.astype(jnp.bfloat16)
        for tile in range(tiles):
            at = place * tiles + tile
            for z in range(NZ):
                out[at // 4 * NZ + z, :, (at % 4) * LANES : (at % 4 + 1) * LANES] = kept[
                    :, tile * LANES : (tile + 1) * LANES
                ]
    for z in range(NZ):
        out[3 * NZ + z, :, 3 * LANES :] = jnp.zeros((rows, LANES), jnp.bfloat16)


def prune(weight, keep):
    rows = weight.shape[0]
    return pl.pallas_call(
        prune_kernel,
        out_shape=jax.ShapeDtypeStruct((NX * NZ, rows, QUARTER), jnp.bfloat16),
        in_specs=[ANY, ANY],
        out_specs=VMEM,
        scratch_shapes=[
            pltpu.VMEM((3, rows, weight.shape[2]), weight.dtype),
            pltpu.VMEM((keep.shape[1], rows), keep.dtype),
            pltpu.SemaphoreType.DMA((2,)),
        ],
        compiler_params=params(),
        name="prune",
    )(jnp.transpose(weight, (1, 0, 2)), keep.T)


def norm_kernel(tokens, gain, after, out):
    del after
    value = tokens[...].astype(jnp.float32)
    meansq = jnp.mean(value * value, axis=1, keepdims=True)
    out[...] = (value * lax.rsqrt(meansq + 1e-06) * gain[...]).astype(jnp.bfloat16)


def norm(tokens, gain, after):
    rows, width = tokens.shape
    step = 32
    return pl.pallas_call(
        norm_kernel,
        out_shape=jax.ShapeDtypeStruct((rows, width), jnp.bfloat16),
        grid=(rows // step,),
        in_specs=[
            pl.BlockSpec((step, width), lambda i: (i, 0)),
            pl.BlockSpec((1, width), lambda i: (0, 0)),
            ANY,
        ],
        out_specs=pl.BlockSpec((step, width), lambda i: (i, 0)),
        compiler_params=params(),
        name="norm",
    )(tokens, gain.reshape(1, width), after)


def bias_kernel(place, line, out):
    rows, columns = out.shape[1:]
    column = lax.broadcasted_iota(jnp.int32, (rows, columns), 1)
    near = jnp.abs(column - TOK - lax.broadcasted_iota(jnp.int32, (rows, columns), 0)) <= RADIUS
    shut = ((column < TOK) & (place[0] == 0)) | ((column >= 2 * TOK) & (place[0] == place[1]))
    allowed = near & ~shut
    for head in range(line.shape[0]):
        block = jnp.broadcast_to(line[head : head + 1, :], (rows, columns))
        block = pltpu.roll(block, 0, 1, stride=1, stride_axis=0)
        out[head] = jnp.where(allowed, block, -jnp.inf)


def bias_blocks(place, position_bias):
    heads = position_bias.shape[1]
    offsets = np.arange(3 * TOK) - TOK
    onehot = buckets(offsets)[None, :] == np.arange(NUM_BUCKETS)[:, None]
    line = jnp.dot(
        position_bias.T,
        jnp.asarray(onehot.astype(np.float32)),
        precision=lax.Precision.HIGHEST,
    )
    return pl.pallas_call(
        bias_kernel,
        out_shape=jax.ShapeDtypeStruct((heads, TOK, 3 * TOK), jnp.float32),
        in_specs=[SMEM, VMEM],
        out_specs=VMEM,
        compiler_params=params(),
        name="bias",
    )(place, line)


def project_kernel(at, *refs):
    tokens, weight, out = refs[:5], refs[5], refs[6]
    toks, rows, total, tok_sem, row_sem = refs[7:]
    x = at[0]
    depth = toks.shape[1] // NX
    copies = []
    for block in range(NX):
        start = 0
        cut = pl.ds(block * depth, depth)
        for i, ref in enumerate(tokens):
            size = ref.shape[0]
            target = toks.at[pl.ds(start, size), cut]
            copies.append(pltpu.make_async_copy(ref.at[:, cut], target, tok_sem.at[block, i]))
            start += size
        for z in range(NZ):
            source = weight.at[:, :, block, z]
            copies.append(
                pltpu.make_async_copy(source, rows.at[block, :, z], row_sem.at[block, z])
            )
    for copy in copies:
        copy.start()
    for block in range(NX):
        for copy in copies[7 * block : 7 * block + 7]:
            copy.wait()
        product = jnp.dot(
            toks[:, block * depth : (block + 1) * depth],
            rows[block].reshape(depth, QUARTER),
            preferred_element_type=jnp.float32,
        )
        if block == 0:
            total[...] = product
        elif block < NX - 1:
            total[...] += product
        else:
            product = (total[...] + product).astype(jnp.bfloat16)
            for d, step in enumerate((0, 3, 1, 2)):
                out[lax.rem(x + step, NX)] = product[d * TOK : (d + 1) * TOK]


def project(at, tokens, weight):
    width = tokens[0].shape[1]
    return pl.pallas_call(
        project_kernel,
        out_shape=jax.ShapeDtypeStruct((NX, TOK, QUARTER), jnp.bfloat16),
        in_specs=[SMEM] + [ANY] * 6,
        out_specs=VMEM,
        scratch_shapes=[
            pltpu.VMEM((NX * TOK, width), jnp.bfloat16),
            pltpu.VMEM((NX, NY, NZ, NC, 32, QUARTER), jnp.bfloat16),
            pltpu.VMEM((NX * TOK, QUARTER), jnp.float32),
            pltpu.SemaphoreType.DMA((NX, 5)),
            pltpu.SemaphoreType.DMA((NX, NZ)),
        ],
        compiler_params=params(58),
        cost_estimate=pl.CostEstimate(
            flops=2 * NX * TOK * width * QUARTER, bytes_accessed=10 << 20, transcendentals=0
        ),
        name="project",
    )(at, *tokens, weight.reshape(NY, NC, NX, NZ, 32, QUARTER))


def own_tile(own, tile):
    return own[tile // 4, :, (tile % 4) * LANES : (tile % 4 + 1) * LANES]


def pair_scores(own, keys, bias, pair, tiles):
    query = own_tile(own, 2 * tiles + pair)
    low = lax.broadcasted_iota(jnp.int32, query.shape, 1) < HS
    for half in range(2):
        picked = jnp.where(low if half == 0 else ~low, query, jnp.zeros_like(query))
        scores = lax.dot_general(
            picked, keys, (((1,), (1,)), ((), ())), preferred_element_type=jnp.float32
        )
        yield scores + bias(2 * pair + half)


def near_kernel(at, own, inner, bias, sums, total, top):
    c = at[0]
    tiles = bias.shape[0] // 2
    low = lax.broadcasted_iota(jnp.int32, (TOK, LANES), 1) < HS
    there = pl.multiple_of((1 - c) * 2 * TOK, TOK)

    def both(tile):
        cut = slice(tile * LANES, (tile + 1) * LANES)
        return jnp.concatenate([own_tile(own, tile), inner[1 - c, :, cut]], axis=0)

    def near_bias(head):
        return jnp.concatenate(
            [bias[head, :, TOK : 2 * TOK], bias[head, :, pl.ds(there, TOK)]], axis=1
        )

    for pair in range(tiles):
        keys, values, results = both(pair), both(tiles + pair), []
        for half, scores in enumerate(pair_scores(own, keys, near_bias, pair, tiles)):
            greatest = jnp.max(scores, axis=1, keepdims=True)
            weights = jnp.exp(scores - greatest)
            top[2 * pair + half] = jnp.broadcast_to(greatest, (TOK, LANES))
            total[2 * pair + half] = jnp.broadcast_to(
                jnp.sum(weights, axis=1, keepdims=True), (TOK, LANES)
            )
            results.append(
                jnp.dot(weights.astype(jnp.bfloat16), values, preferred_element_type=jnp.float32)
            )
        sums[:, pair * LANES : (pair + 1) * LANES] = jnp.where(low, *results)


def attend_kernel(at, own, outer, bias, sums, total, top, out, held, sem):
    copies = []
    c = at[0]
    tiles = bias.shape[0] // 2
    low = lax.broadcasted_iota(jnp.int32, (TOK, LANES), 1) < HS
    there = pl.multiple_of(c * 2 * TOK, TOK)
    for pair in range(tiles):
        cut = slice(pair * LANES, (pair + 1) * LANES)
        keys = outer[:, cut]
        values = outer[:, (tiles + pair) * LANES : (tiles + pair + 1) * LANES]
        scales, totals, results = [], [], []
        far_bias = lambda head: bias[head, :, pl.ds(there, TOK)]
        for half, scores in enumerate(pair_scores(own, keys, far_bias, pair, tiles)):
            head = 2 * pair + half
            greatest = jnp.maximum(top[head], jnp.max(scores, axis=1, keepdims=True))
            weights = jnp.exp(scores - greatest)
            scales.append(jnp.exp(top[head] - greatest))
            totals.append(total[head] * scales[-1] + jnp.sum(weights, axis=1, keepdims=True))
            results.append(
                jnp.dot(weights.astype(jnp.bfloat16), values, preferred_element_type=jnp.float32)
            )
        summed = sums[:, cut] * jnp.where(low, *scales) + jnp.where(low, *results)
        held[:, cut] = (summed / jnp.where(low, *totals)).astype(jnp.bfloat16)
        copies.append(pltpu.make_async_copy(held.at[:, cut], out.at[:, cut], sem.at[pair]))
        copies[-1].start()
    for copy in copies:
        copy.wait()


def attend(core, own, inner, outer, bias):
    heads = bias.shape[0]
    row = jax.ShapeDtypeStruct((heads, TOK, LANES), jnp.float32)
    near = pl.pallas_call(
        near_kernel,
        out_shape=[jax.ShapeDtypeStruct((TOK, heads * HS), jnp.float32), row, row],
        in_specs=[SMEM] + [VMEM] * 3,
        out_specs=[VMEM] * 3,
        compiler_params=params(),
        name="near",
    )(core, own, inner, bias)
    return pl.pallas_call(
        attend_kernel,
        out_shape=jax.ShapeDtypeStruct((TOK, heads * HS), jnp.bfloat16),
        in_specs=[SMEM] + [VMEM] * 6,
        out_specs=ANY,
        scratch_shapes=[
            pltpu.VMEM((TOK, heads * HS), jnp.bfloat16),
            pltpu.SemaphoreType.DMA((heads // 2,)),
        ],
        compiler_params=params(),
        name="attend",
    )(core, own, outer, bias, *near)


def shifted(count, step):
    return [(i, (i + step) % count) for i in range(count)]


def body(tokens, norm_gain, qkv_weight, qkv_keep, position_bias):
    x, c = lax.axis_index("x"), lax.axis_index("c")
    seq, last = lax.axis_index(SEQ), lax.axis_size(SEQ) - 1
    pruned = prune(qkv_weight, qkv_keep)
    mine = lax.all_to_all(pruned, ("x", "zh"), 0, 0, tiled=True)
    normed = norm(tokens, norm_gain, mine[0, :16, :LANES])
    behind, ahead = (lax.ppermute(normed, "x", shifted(NX, d)) for d in (1, 3))
    half = normed.shape[0] // 2
    far = [lax.ppermute(behind[:half], "x", shifted(NX, 1))]
    far += [lax.ppermute(ahead[half:], "x", shifted(NX, 3))]
    gathered = lax.all_gather(mine.reshape(-1, QUARTER), ("y", "c"), axis=0, tiled=True)
    bias = bias_blocks(jnp.stack([seq, jnp.int32(last)]).astype(jnp.int32), position_bias)
    at = x.reshape(1).astype(jnp.int32)
    projected = project(at, [normed, behind, ahead, *far], gathered)
    own = lax.all_to_all(projected, "x", 0, 0, tiled=True)
    edges = jnp.concatenate([own[0], own[1], own[2][:, : QUARTER // 2]], axis=1)
    inner = lax.all_gather(edges, "c")
    pairs = [(i, i + 1) for i in range(1, last, 2)]
    outer = lax.ppermute(edges, SEQ, pairs + [(j, i) for i, j in pairs])
    return attend(c.reshape(1).astype(jnp.int32), own, inner, outer, bias)


def solution(mesh):
    grid = Mesh(mesh.devices.reshape(NX, NY, NZ, NC, NT), SEQ + ("tp",))
    return jax.shard_map(
        body,
        mesh=grid,
        in_specs=(P(SEQ, None), P(), P(SEQ, None, "tp"), P(SEQ, "tp"), P(None, "tp")),
        out_specs=P(SEQ, "tp"),
        check_vma=False,
    )
```

```python
import functools

import jax
import jax.numpy as jnp
import numpy as np
from jax import lax
from jax.experimental import pallas as pl
from jax.experimental.pallas import tpu as pltpu
from jax.sharding import Mesh, PartitionSpec as P

HS = 64
RADIUS = 127
NUM_BUCKETS = 32
MAX_DIST = 128
LANES = 128
TOK = 128
NX, NY, NZ, NC, NT = 4, 8, 2, 2, 4
SEQ = ("x", "y", "zh", "c")
QUARTER = 512
VMEM = pl.BlockSpec(memory_space=pltpu.VMEM)
SMEM = pl.BlockSpec(memory_space=pltpu.SMEM)
ANY = pl.BlockSpec(memory_space=pl.ANY)


def buckets(offsets):
    offsets = np.asarray(offsets, np.int64)
    half_count = NUM_BUCKETS // 2
    sign_part = (offsets > 0).astype(np.int64) * half_count
    distance = np.abs(offsets)
    exact_count = half_count // 2
    log_bucket = exact_count + (
        np.log(np.maximum(distance, 1) / exact_count)
        / np.log(MAX_DIST / exact_count)
        * (half_count - exact_count)
    ).astype(np.int64)
    log_bucket = np.minimum(log_bucket, half_count - 1)
    return sign_part + np.where(distance < exact_count, distance, log_bucket)


def params(mib=8):
    return pltpu.CompilerParams(vmem_limit_bytes=mib * 1024 * 1024)


def prune_kernel(given_weight, given_keep, out, weight, keep, sem):
    copies = [
        pltpu.make_async_copy(given_keep, keep, sem.at[0]),
        pltpu.make_async_copy(given_weight, weight, sem.at[1]),
    ]
    for copy in copies:
        copy.start()
    for copy in copies:
        copy.wait()
    rows, cols = weight.shape[1:]
    words = keep[...].T
    lane = lax.broadcasted_iota(jnp.int32, (rows, cols), 1)
    part, head = (lane >> 4) & 3, lane >> 6
    word = jnp.broadcast_to(words[:, 3:4], (rows, cols))
    for j in range(3):
        word = jnp.where(part == j, words[:, j : j + 1], word)
    tiles = cols // LANES
    for place, matrix in enumerate((1, 2, 0)):
        flag = (word >> (head + 10 * matrix)) & 1
        kept = weight[matrix].astype(jnp.float32) * flag.astype(jnp.float32)
        kept = kept.astype(jnp.bfloat16)
        for tile in range(tiles):
            at = place * tiles + tile
            for z in range(NZ):
                out[at // 4 * NZ + z, :, (at % 4) * LANES : (at % 4 + 1) * LANES] = kept[
                    :, tile * LANES : (tile + 1) * LANES
                ]
    for z in range(NZ):
        out[3 * NZ + z, :, 3 * LANES :] = jnp.zeros((rows, LANES), jnp.bfloat16)


def prune(weight, keep):
    rows = weight.shape[0]
    return pl.pallas_call(
        prune_kernel,
        out_shape=jax.ShapeDtypeStruct((NX * NZ, rows, QUARTER), jnp.bfloat16),
        in_specs=[ANY, ANY],
        out_specs=VMEM,
        scratch_shapes=[
            pltpu.VMEM((3, rows, weight.shape[2]), weight.dtype),
            pltpu.VMEM((keep.shape[1], rows), keep.dtype),
            pltpu.SemaphoreType.DMA((2,)),
        ],
        compiler_params=params(),
        name="prune",
    )(jnp.transpose(weight, (1, 0, 2)), keep.T)


def norm_kernel(tokens, gain, after, low, high):
    del after
    half = low.shape[0]
    for start in range(0, 2 * half, 32):
        value = tokens[start : start + 32, :].astype(jnp.float32)
        meansq = jnp.mean(value * value, axis=1, keepdims=True)
        value = (value * lax.rsqrt(meansq + 1e-06) * gain[...]).astype(jnp.bfloat16)
        out = low if start < half else high
        out[start % half : start % half + 32, :] = value


def norm(tokens, gain, after):
    rows, width = tokens.shape
    return pl.pallas_call(
        norm_kernel,
        out_shape=[jax.ShapeDtypeStruct((rows // 2, width), jnp.bfloat16)] * 2,
        in_specs=[VMEM, VMEM, ANY],
        out_specs=[VMEM] * 2,
        compiler_params=params(),
        name="norm",
    )(tokens, gain.reshape(1, width), after)


def bias_kernel(place, line, out):
    rows, columns = out.shape[1:]
    column = lax.broadcasted_iota(jnp.int32, (rows, columns), 1)
    near = jnp.abs(column - TOK - lax.broadcasted_iota(jnp.int32, (rows, columns), 0)) <= RADIUS
    shut = ((column < TOK) & (place[0] == 0)) | ((column >= 2 * TOK) & (place[0] == place[1]))
    allowed = near & ~shut
    for head in range(line.shape[0]):
        block = jnp.broadcast_to(line[head : head + 1, :], (rows, columns))
        block = pltpu.roll(block, 0, 1, stride=1, stride_axis=0)
        out[head] = jnp.where(allowed, block, -jnp.inf)


def bias_blocks(place, position_bias):
    heads = position_bias.shape[1]
    offsets = np.arange(3 * TOK) - TOK
    onehot = buckets(offsets)[None, :] == np.arange(NUM_BUCKETS)[:, None]
    line = jnp.dot(
        position_bias.T,
        jnp.asarray(onehot.astype(np.float32)),
        precision=lax.Precision.HIGHEST,
    )
    return pl.pallas_call(
        bias_kernel,
        out_shape=jax.ShapeDtypeStruct((heads, TOK, 3 * TOK), jnp.float32),
        in_specs=[SMEM, VMEM],
        out_specs=VMEM,
        compiler_params=params(),
        name="bias",
    )(place, line)


def project_kernel(at, *refs):
    tokens, weight, out = refs[:8], refs[8], refs[9]
    toks, rows, total, tok_sem, row_sem = refs[10:]
    x = at[0]
    depth = toks.shape[1] // NX
    copies = []
    for block in range(NX):
        start = 0
        cut = pl.ds(block * depth, depth)
        for i, ref in enumerate(tokens):
            size = ref.shape[0]
            target = toks.at[pl.ds(start, size), cut]
            copies.append(pltpu.make_async_copy(ref.at[:, cut], target, tok_sem.at[block, i]))
            start += size
        for z in range(NZ):
            source = weight.at[:, :, block, z]
            copies.append(
                pltpu.make_async_copy(source, rows.at[block, :, z], row_sem.at[block, z])
            )
    for copy in copies:
        copy.start()
    for block in range(NX):
        for copy in copies[10 * block : 10 * block + 10]:
            copy.wait()
        product = jnp.dot(
            toks[:, block * depth : (block + 1) * depth],
            rows[block].reshape(depth, QUARTER),
            preferred_element_type=jnp.float32,
        )
        if block == 0:
            total[...] = product
        elif block < NX - 1:
            total[...] += product
        else:
            product = (total[...] + product).astype(jnp.bfloat16)
            for d, step in enumerate((0, 3, 1, 2)):
                out[lax.rem(x + step, NX)] = product[d * TOK : (d + 1) * TOK]


def project(at, tokens, weight):
    width = tokens[0].shape[1]
    return pl.pallas_call(
        project_kernel,
        out_shape=jax.ShapeDtypeStruct((NX, TOK, QUARTER), jnp.bfloat16),
        in_specs=[SMEM] + [ANY] * 9,
        out_specs=VMEM,
        scratch_shapes=[
            pltpu.VMEM((NX * TOK, width), jnp.bfloat16),
            pltpu.VMEM((NX, NY, NZ, NC, 32, QUARTER), jnp.bfloat16),
            pltpu.VMEM((NX * TOK, QUARTER), jnp.float32),
            pltpu.SemaphoreType.DMA((NX, 8)),
            pltpu.SemaphoreType.DMA((NX, NZ)),
        ],
        compiler_params=params(58),
        cost_estimate=pl.CostEstimate(
            flops=2 * NX * TOK * width * QUARTER, bytes_accessed=10 << 20, transcendentals=0
        ),
        name="project",
    )(at, *tokens, weight.reshape(NY, NC, NX, NZ, 32, QUARTER))


def own_tile(own, tile):
    return own[tile // 4, :, (tile % 4) * LANES : (tile % 4 + 1) * LANES]


def pair_scores(own, keys, bias, pair, tiles):
    query = own_tile(own, 2 * tiles + pair)
    low = lax.broadcasted_iota(jnp.int32, query.shape, 1) < HS
    for half in range(2):
        picked = jnp.where(low if half == 0 else ~low, query, jnp.zeros_like(query))
        scores = lax.dot_general(
            picked, keys, (((1,), (1,)), ((), ())), preferred_element_type=jnp.float32
        )
        yield scores + bias(2 * pair + half)


def near_kernel(at, own, inner, bias, sums, total, top):
    c = at[0]
    tiles = bias.shape[0] // 2
    low = lax.broadcasted_iota(jnp.int32, (TOK, LANES), 1) < HS
    there = pl.multiple_of((1 - c) * 2 * TOK, TOK)

    def both(tile):
        cut = slice(tile * LANES, (tile + 1) * LANES)
        return jnp.concatenate([own_tile(own, tile), inner[1 - c, :, cut]], axis=0)

    def near_bias(head):
        return jnp.concatenate(
            [bias[head, :, TOK : 2 * TOK], bias[head, :, pl.ds(there, TOK)]], axis=1
        )

    for pair in range(tiles):
        keys, values, results = both(pair), both(tiles + pair), []
        for half, scores in enumerate(pair_scores(own, keys, near_bias, pair, tiles)):
            greatest = jnp.max(scores, axis=1, keepdims=True)
            weights = jnp.exp(scores - greatest)
            top[2 * pair + half] = jnp.broadcast_to(greatest, (TOK, LANES))
            total[2 * pair + half] = jnp.broadcast_to(
                jnp.sum(weights, axis=1, keepdims=True), (TOK, LANES)
            )
            results.append(
                jnp.dot(weights.astype(jnp.bfloat16), values, preferred_element_type=jnp.float32)
            )
        sums[:, pair * LANES : (pair + 1) * LANES] = jnp.where(low, *results)


def attend_kernel(at, own, far_keys, far_values, bias, sums, total, top, out, held, sem):
    copies = []
    c = at[0]
    tiles = bias.shape[0] // 2
    low = lax.broadcasted_iota(jnp.int32, (TOK, LANES), 1) < HS
    there = pl.multiple_of(c * 2 * TOK, TOK)
    for pair in range(tiles):
        cut = slice(pair * LANES, (pair + 1) * LANES)
        keys, values = far_keys[:, cut], far_values[:, cut]
        scales, totals, results = [], [], []
        far_bias = lambda head: bias[head, :, pl.ds(there, TOK)]
        for half, scores in enumerate(pair_scores(own, keys, far_bias, pair, tiles)):
            head = 2 * pair + half
            greatest = jnp.maximum(top[head], jnp.max(scores, axis=1, keepdims=True))
            weights = jnp.exp(scores - greatest)
            scales.append(jnp.exp(top[head] - greatest))
            totals.append(total[head] * scales[-1] + jnp.sum(weights, axis=1, keepdims=True))
            results.append(
                jnp.dot(weights.astype(jnp.bfloat16), values, preferred_element_type=jnp.float32)
            )
        summed = sums[:, cut] * jnp.where(low, *scales) + jnp.where(low, *results)
        held[:, cut] = (summed / jnp.where(low, *totals)).astype(jnp.bfloat16)
        copies.append(pltpu.make_async_copy(held.at[:, cut], out.at[:, cut], sem.at[pair]))
        copies[-1].start()
    for copy in copies:
        copy.wait()


def attend(core, own, inner, outer, bias):
    heads = bias.shape[0]
    row = jax.ShapeDtypeStruct((heads, TOK, LANES), jnp.float32)
    near = pl.pallas_call(
        near_kernel,
        out_shape=[jax.ShapeDtypeStruct((TOK, heads * HS), jnp.float32), row, row],
        in_specs=[SMEM] + [VMEM] * 3,
        out_specs=[VMEM] * 3,
        compiler_params=params(),
        name="near",
    )(core, own, inner, bias)
    return pl.pallas_call(
        attend_kernel,
        out_shape=jax.ShapeDtypeStruct((TOK, heads * HS), jnp.bfloat16),
        in_specs=[SMEM] + [VMEM] * 7,
        out_specs=ANY,
        scratch_shapes=[
            pltpu.VMEM((TOK, heads * HS), jnp.bfloat16),
            pltpu.SemaphoreType.DMA((heads // 2,)),
        ],
        compiler_params=params(),
        name="attend",
    )(core, own, *outer, bias, *near)


def shifted(count, step):
    return [(i, (i + step) % count) for i in range(count)]


def body(tokens, norm_gain, qkv_weight, qkv_keep, position_bias):
    x, c = lax.axis_index("x"), lax.axis_index("c")
    seq, last = lax.axis_index(SEQ), lax.axis_size(SEQ) - 1
    pruned = prune(qkv_weight, qkv_keep)
    mine = lax.all_to_all(pruned, ("x", "zh"), 0, 0, tiled=True)
    low, high = norm(tokens, norm_gain, pruned)
    behind_low = lax.ppermute(low, "x", shifted(NX, 1))
    ahead_high = lax.ppermute(high, "x", shifted(NX, 3))
    far_low = lax.ppermute(behind_low, "x", shifted(NX, 1))
    far_high = lax.ppermute(ahead_high, "x", shifted(NX, 3))
    behind_high = lax.ppermute(high, "x", shifted(NX, 1))
    ahead_low = lax.ppermute(low, "x", shifted(NX, 3))
    pieces = [low, high, behind_low, behind_high, ahead_low, ahead_high, far_low, far_high]
    gathered = lax.all_gather(mine.reshape(-1, QUARTER), ("y", "c"), axis=0, tiled=True)
    bias = bias_blocks(jnp.stack([seq, jnp.int32(last)]).astype(jnp.int32), position_bias)
    at = x.reshape(1).astype(jnp.int32)
    projected = project(at, pieces, gathered)
    own = lax.all_to_all(projected, "x", 0, 0, tiled=True)
    edges = jnp.concatenate([own[0], own[1], own[2][:, : QUARTER // 2]], axis=1)
    inner = lax.all_gather(edges, "c")
    pairs = [(i, i + 1) for i in range(1, last, 2)]
    pairs += [(j, i) for i, j in pairs]
    width = edges.shape[1] // 2
    outer = [lax.ppermute(part, SEQ, pairs) for part in (edges[:, :width], edges[:, width:])]
    return attend(c.reshape(1).astype(jnp.int32), own, inner, outer, bias)


def solution(mesh):
    grid = Mesh(mesh.devices.reshape(NX, NY, NZ, NC, NT), SEQ + ("tp",))
    return jax.shard_map(
        body,
        mesh=grid,
        in_specs=(P(SEQ, None), P(), P(SEQ, None, "tp"), P(SEQ, "tp"), P(None, "tp")),
        out_specs=P(SEQ, "tp"),
        check_vma=False,
    )
```
